32 devices in a mesh: groups: 2 (over x), dp: 8 (over z, y), tensor: 2 (over core).
Axes of the slice: x: 2, y: 2, z: 4, core: 2. Of those that a mesh axis runs over, the one named last changes fastest.
Arguments:
- normed_hidden_states: bfloat16 [4096, 8192], P(('groups', 'dp'), 'tensor'), parts along dimension 0, may hold values from -6 to 6
- value_base_matrix: bfloat16 [8192, 1024], P('tensor'), may hold values from -0.0625 to 0.0625
- down_factor_slots: bfloat16 [512, 64, 8192], P(('groups', 'dp'), None, 'tensor'), parts along dimension 0, may hold values from -0.0625 to 0.0625
- up_factor_slots: bfloat16 [512, 64, 1024], P(('groups', 'dp'), None, 'tensor'), parts along dimension 0, may hold values from -0.75 to 0.75
- row_adapter_index: int32 [4096], P(('groups', 'dp')), parts along dimension 0, may hold values from 0 to 255, as said below
- adapter_slot_table: int32 [512], P('groups'), parts along dimension 0, may hold values from 0 to 255, as said below
Outputs:
- projected: bfloat16 [4096, 1024], P(('groups', 'dp'), 'tensor'), parts along dimension 0
The draws below stay inside these ranges and needn't reach their ends.
There are 2 independent parts, one for each index of `groups`. The reference program is written for one: setup_inputs(seed, part) draws one part's arguments, and reference() takes and returns one part's arrays. A program takes and returns all parts, laid end to end along the dimension named above; an argument that names none is the same for every part. Nothing has to cross between parts.
Inputs may be any that keep to these rules, and one draw needn't show every extreme that they name: `row_adapter_index`: the ids of one device's 256 rows (an aligned block) do not fall. Call slots k * 32 to (k + 1) * 32 - 1 the k-th slot block: at most 128 rows of one aligned block have adapters whose slot lies in one slot block, and in every draw some slot block has exactly 128 rows in every aligned block. `adapter_slot_table`: each slot holds exactly one adapter.
All inputs are finite; a program needn't handle non-finite values.
Results may differ from the reference program's by a relative error of at most 0.005.
Values may be sent and summed in bfloat16 or wider, within the bound.
No kernel may reach another device: no remote copies, remote signals or barrier semaphores. Data moves between devices by JAX's collectives and lax.ppermute only.
A program may use at most 192 MiB of HBM per device.

```python
import jax
import jax.numpy as jnp
from jax import lax

MODEL_WIDTH = 8192
VALUE_OUTPUTS = 1024
ADAPTER_RANK = 64
ADAPTER_TOTAL = 256
ROWS_DEV = 256
CAP = 128
ROWS = 2048
N_DP = 8


def shared_routing(key):
    subkeys = jax.random.split(key, 5)
    slot_table = jax.random.permutation(subkeys[0], ADAPTER_TOTAL).astype(jnp.int32)
    adapter_at = jnp.argsort(slot_table, stable=True).astype(jnp.int32)
    per_owner = ADAPTER_TOTAL // N_DP
    capacity = 4 * ROWS_DEV // N_DP
    positions = N_DP * capacity
    busiest = jax.random.randint(subkeys[1], (), 0, N_DP)
    popularity = jax.random.randint(subkeys[2], (N_DP,), 1, 9)
    jitter = jax.random.randint(subkeys[3], (N_DP, positions), 0, 4096)
    slot_owner = jnp.arange(positions, dtype=jnp.int32) // capacity
    offsets = jnp.arange(positions, dtype=jnp.int32)[None, :]
    scores = popularity[slot_owner][None, :] * jitter * positions + offsets
    scores = jnp.where(slot_owner[None, :] == busiest, 2 ** 30 + offsets, scores).astype(jnp.int32)
    picked_slots = lax.top_k(scores, ROWS_DEV)[1].astype(jnp.int32)
    owners = picked_slots // capacity
    within = jax.random.randint(subkeys[4], (N_DP, ROWS_DEV), 0, per_owner)
    drawn_ids = adapter_at[owners * per_owner + within]
    drawn_ids = jnp.sort(drawn_ids, axis=1).reshape(N_DP * ROWS_DEV)
    return (slot_table, drawn_ids.astype(jnp.int32))


def draw_row_adapter_index(key, part):
    return shared_routing(key)[1]


def draw_adapter_slot_table(key, part):
    return shared_routing(key)[0]


def block_scale(own_key, extent, pieces, least, top_value):
    gain, own = 1.0, jax.random.fold_in(own_key, 6)
    for position, blocks in pieces:
        draws = jnp.exp(jax.random.uniform(jax.random.fold_in(own, position), (blocks,), jnp.float32, least / len(pieces), top_value / len(pieces)))
        gain = gain * jnp.repeat(draws, extent[position] // blocks).reshape([-1 if axis == position else 1 for axis in range(len(extent))])
    return gain


def scatter_about(own_key, extent, spread, reach, pieces=(), held_as=jnp.bfloat16):
    gain = block_scale(own_key, extent, pieces, -0.22, 0.18) if pieces else 1.0
    result = jax.random.normal(own_key, extent, jnp.float32) * spread * gain
    return jnp.minimum(jnp.maximum(result, -reach), reach).astype(held_as)


def setup_inputs(seed: int = 0, part: int = 0) -> dict:
    seeds = jax.random.split(jax.random.key(seed), 7)
    part_splits = jax.random.split(jax.random.fold_in(seeds[6], part), 7)
    normed_hidden_states = scatter_about(part_splits[0], (ROWS, MODEL_WIDTH), 1.0, 6.0, ((0, 8), (1, 2)))
    value_base_matrix = scatter_about(seeds[1], (MODEL_WIDTH, VALUE_OUTPUTS), MODEL_WIDTH ** -0.5, 0.0625, ((0, 2),))
    down_factor_slots = scatter_about(part_splits[2], (ADAPTER_TOTAL, ADAPTER_RANK, MODEL_WIDTH), MODEL_WIDTH ** -0.5, 0.0625, ((0, 8), (2, 2)))
    up_factor_slots = scatter_about(part_splits[3], (ADAPTER_TOTAL, ADAPTER_RANK, VALUE_OUTPUTS), ADAPTER_RANK ** -0.5, 0.75, ((0, 8), (2, 2)))
    row_adapter_index = draw_row_adapter_index(jax.random.fold_in(jax.random.fold_in(seeds[6], part), 71), part)
    adapter_slot_table = draw_adapter_slot_table(jax.random.fold_in(jax.random.fold_in(seeds[6], part), 71), part)
    return dict(normed_hidden_states=normed_hidden_states, value_base_matrix=value_base_matrix, down_factor_slots=down_factor_slots, up_factor_slots=up_factor_slots, row_adapter_index=row_adapter_index, adapter_slot_table=adapter_slot_table)


def reference(normed_hidden_states, value_base_matrix, down_factor_slots, up_factor_slots, row_adapter_index, adapter_slot_table):
    row_count = normed_hidden_states.shape[0]
    slot_ids = adapter_slot_table[row_adapter_index].astype(jnp.int32)
    base_sum = jnp.dot(normed_hidden_states, value_base_matrix, preferred_element_type=jnp.float32)
    row_order = jnp.argsort(slot_ids, stable=True).astype(jnp.int32)
    sorted_slots = slot_ids[row_order]
    ordered = normed_hidden_states[row_order]
    window = N_DP * CAP
    slot_range = jnp.arange(ADAPTER_TOTAL, dtype=jnp.int32)
    starts = jnp.searchsorted(sorted_slots, slot_range, side="left").astype(jnp.int32)
    finish = jnp.searchsorted(sorted_slots, slot_range, side="right").astype(jnp.int32)
    padded = jnp.concatenate([ordered, jnp.zeros((window, MODEL_WIDTH), normed_hidden_states.dtype)], axis=0)

    def accumulate(factor_slot_index, totals):
        first_row = starts[factor_slot_index]
        rows_in_block = lax.dynamic_slice_in_dim(padded, first_row, window, 0)
        rank_projection = lax.dot_general(rows_in_block, down_factor_slots[factor_slot_index], (((1,), (1,)), ((), ())),
                                   preferred_element_type=jnp.float32).astype(jnp.bfloat16)
        adapter_row_update = jnp.dot(rank_projection, up_factor_slots[factor_slot_index], preferred_element_type=jnp.float32).astype(jnp.bfloat16)
        live_rows = jnp.arange(window, dtype=jnp.int32) < (finish[factor_slot_index] - first_row)
        current = lax.dynamic_slice_in_dim(totals, first_row, window, 0)
        current = current + jnp.where(live_rows[:, None], adapter_row_update.astype(jnp.float32), jnp.float32(0.0))
        return lax.dynamic_update_slice_in_dim(totals, current, first_row, 0)

    totals = lax.fori_loop(0, ADAPTER_TOTAL, accumulate, jnp.zeros((row_count + window, VALUE_OUTPUTS), jnp.float32))
    adapter_row_update = jnp.zeros((row_count, VALUE_OUTPUTS), jnp.float32).at[row_order].set(totals[:row_count])
    return (base_sum + adapter_row_update).astype(jnp.bfloat16)
```

```python
import functools

import jax
import jax.numpy as jnp
from jax import lax
from jax.experimental import pallas as pl
from jax.experimental.pallas import tpu as pltpu
from jax.sharding import PartitionSpec as P

SLOTS_A_STEP = 8
VMEM_BYTES = 48 * 1024 * 1024
LAST = (((1,), (1,)), ((), ()))
FIRST = (((0,), (0,)), ((), ()))


def ranks_kernel(layout, rank, *refs):
    pieces = refs[: len(layout)]
    slot_ref, factors_ref, out_ref, rows_ref = refs[len(layout) :]
    step = pl.program_id(0)
    slots = factors_ref.shape[0] // rank

    @pl.when(step == 0)
    def _():
        out_ref[...] = jnp.zeros_like(out_ref)
        for (row, column), piece in zip(layout, pieces):
            height, width = piece.shape
            rows_ref[row : row + height, column : column + width] = piece[...]

    products = lax.dot_general(
        factors_ref[...], rows_ref[...], LAST, preferred_element_type=jnp.float32
    )
    slot_of_row = slot_ref[...]
    kept = out_ref[...]
    for slot in range(slots):
        kept = jnp.where(
            slot_of_row == step * slots + slot, products[slot * rank : (slot + 1) * rank], kept
        )
    out_ref[...] = kept


def picked_ranks(pieces, slots, factors, rank, column_block=0):
    total_rows = slots.shape[0]
    width = max(column + piece.shape[1] for _, column, piece in pieces)
    height = SLOTS_A_STEP * rank
    whole = lambda step: (0, 0)
    return pl.pallas_call(
        functools.partial(ranks_kernel, [(row, column) for row, column, _ in pieces], rank),
        grid=(factors.shape[0] // height,),
        out_shape=jax.ShapeDtypeStruct((rank, total_rows), jnp.float32),
        in_specs=[pl.BlockSpec(piece.shape, whole) for _, _, piece in pieces]
        + [
            pl.BlockSpec((1, total_rows), whole),
            pl.BlockSpec((height, width), lambda step: (step, column_block)),
        ],
        out_specs=pl.BlockSpec((rank, total_rows), whole),
        scratch_shapes=[pltpu.VMEM((total_rows, width), jnp.bfloat16)],
        compiler_params=pltpu.CompilerParams(vmem_limit_bytes=VMEM_BYTES),
        cost_estimate=pl.CostEstimate(
            flops=2 * total_rows * factors.shape[0] * width,
            bytes_accessed=2 * (total_rows + factors.shape[0]) * width,
            transcendentals=0,
        ),
    )(*[piece for _, _, piece in pieces], slots[None, :], factors)


def updates_kernel(own_ref, peer_ref, slot_ref, factors_ref, out_ref):
    rank = own_ref.shape[0]
    low = (own_ref[...] + peer_ref[...]).astype(jnp.bfloat16).astype(jnp.float32)
    slot_of_row = slot_ref[...]
    spread = jnp.concatenate(
        [
            jnp.where(slot_of_row == slot, low, 0.0).astype(jnp.bfloat16)
            for slot in range(factors_ref.shape[0] // rank)
        ],
        axis=0,
    )
    out_ref[...] = lax.dot_general(
        spread, factors_ref[...], FIRST, preferred_element_type=jnp.float32
    ).astype(out_ref.dtype)


def row_updates(partial_low, slots, factors):
    other = lax.ppermute(partial_low, "tensor", [(0, 1), (1, 0)])
    rows, columns = slots.shape[0], factors.shape[1]
    return pl.pallas_call(
        updates_kernel,
        out_shape=jax.ShapeDtypeStruct((rows, columns), jnp.bfloat16),
        in_specs=[pl.BlockSpec(memory_space=pltpu.VMEM)] * 4,
        out_specs=pl.BlockSpec(memory_space=pltpu.VMEM),
        compiler_params=pltpu.CompilerParams(vmem_limit_bytes=VMEM_BYTES),
        cost_estimate=pl.CostEstimate(
            flops=2 * rows * factors.shape[0] * columns,
            bytes_accessed=2 * factors.shape[0] * columns,
            transcendentals=0,
        ),
    )(partial_low, other, slots[None, :], factors)


def looked_up(ids, table):
    hits = ids[..., None] == jnp.arange(table.shape[0], dtype=jnp.int32)
    return jnp.sum(jnp.where(hits, table, 0), axis=-1)


def after(value, *others):
    return lax.optimization_barrier((value, *others))[0]


def line_relay(hidden, down, up, own_ids, table, rank):
    row_count, width = hidden.shape
    resident = down.shape[0] // rank
    capacity = 4 * row_count // lax.axis_size("dp")
    half = width // 2
    me = lax.axis_index("dp")
    devices = range(8)

    def exchange(value, flip):
        return lax.ppermute(value, "dp", [(i, i ^ flip) for i in devices])

    def middle(value):
        return lax.ppermute(value, "dp", [(i, i ^ 6) for i in devices if i // 2 in (1, 2)])

    def outward(value, flip=0):
        return lax.ppermute(value, "dp", [(i, i ^ 2 ^ flip) for i in devices if i // 2 in (1, 2)])

    ids = lax.all_to_all(jnp.broadcast_to(own_ids, (8, 1, row_count)), "dp", 0, 0, tiled=True)
    ids = ids.reshape(2, 2, 2, row_count)
    for axis, bit in enumerate((4, 2, 1)):
        ids = jnp.where(me & bit != 0, jnp.flip(ids, axis), ids)
    slots = looked_up(ids.reshape(8, row_count), table)

    hidden = after(hidden, ids)
    one, mid = exchange(hidden, 2), middle(hidden)

    pairs = [(0, owner) for owner in devices]
    pairs += [(1, 0), (2, 0), (2, 1), (3, 0), (4, 0), (4, 1), (4, 2), (4, 3), (5, 0), (6, 0), (6, 1), (7, 0)]
    owners = slots // resident
    sources = jnp.stack([owners[source] for source, _ in pairs])
    wanted = jnp.stack([me ^ owner for _, owner in pairs])[:, None]
    hit = sources == wanted
    places = jnp.where(hit, jnp.cumsum(hit.astype(jnp.int32), axis=1) - 1, -1)
    place = {pair: places[n] for n, pair in enumerate(pairs)}
    order = jnp.arange(capacity, dtype=jnp.int32)[:, None]

    def one_hot(place):
        return (order == place[None, :]).astype(jnp.bfloat16)

    def compact(place, piece):
        return jnp.dot(one_hot(place), piece, preferred_element_type=jnp.float32).astype(
            jnp.bfloat16
        )

    def split_rows(source, rows):
        pair = exchange(compact(place[source, 1], rows), 1)
        return [(0, 0, compact(place[source, 0], rows)), (capacity, 0, pair)]

    def compact_slots(*sources):
        local = slots % resident
        lists = [
            jnp.sum(jnp.where(order == place[f, 0][None, :], local[f][None, :] + 1, 0), axis=1) - 1
            for f in sources
        ]
        return jnp.concatenate(lists)

    back = {}
    slots_0, slots_1 = compact_slots(0, 1), compact_slots(2, 3)
    slots_2, slots_3 = compact_slots(4, 5), compact_slots(6, 7)

    rows_0 = split_rows(0, hidden)
    update_0 = row_updates(picked_ranks(rows_0, slots_0, down, rank), slots_0, up)
    back[0], back[1] = update_0[:capacity], exchange(update_0[capacity:], 1)

    edge = (me // 2 == 0) | (me // 2 == 3)
    two = jnp.where(edge, outward(mid), middle(one))

    rows_1 = split_rows(2, one)
    low_1 = picked_ranks(rows_1, after(slots_1, update_0), down, rank)
    update_1 = row_updates(low_1, slots_1, up)
    back[2], back[3] = exchange(update_1[:capacity], 2), exchange(update_1[capacity:], 3)

    rows_mid = split_rows(6, mid)
    low_mid = picked_ranks(rows_mid, after(slots_3, update_1), down, rank)

    def last_hop(rows):
        straight, across = outward(compact(place[4, 2], rows)), outward(compact(place[4, 3], rows), 1)
        return [(0, 0, straight), (capacity, 0, across)]

    rows_3a, rows_3b = last_hop(two[:, :half]), last_hop(two[:, half:])

    rows_2 = split_rows(4, two)
    low_a = picked_ranks(rows_3a, after(slots_3, low_mid), down, rank, 0)
    low_2 = picked_ranks(rows_2, after(slots_2, low_a), down, rank)
    update_2 = row_updates(low_2, slots_2, up)
    back[4], back[5] = exchange(update_2[:capacity], 4), exchange(update_2[capacity:], 5)

    low_b = picked_ranks(rows_3b, after(slots_3, update_2), down, rank, 1)
    update_3 = row_updates(low_mid + low_a + low_b, slots_3, up)
    back[6], back[7] = exchange(update_3[:capacity], 6), exchange(update_3[capacity:], 7)

    def spread_back(owners):
        return lax.dot_general(
            jnp.concatenate([one_hot(place[0, owner]) for owner in owners]),
            jnp.concatenate([back[owner] for owner in owners]),
            FIRST,
            preferred_element_type=jnp.float32,
        )

    return spread_back(range(6)) + spread_back((6, 7))


def all_to_all_relay(hidden, down, up, own_ids, table, rank):
    row_count = hidden.shape[0]
    peers = lax.axis_size("dp")
    resident = down.shape[0] // rank
    capacity = 4 * row_count // peers
    own_slots = looked_up(own_ids, table)
    hits = (own_slots // resident)[:, None] == jnp.arange(peers, dtype=jnp.int32)[None, :]
    place = jnp.sum(jnp.cumsum(hits.astype(jnp.int32), axis=0) * hits, axis=1) - 1
    target = (own_slots // resident) * capacity + place
    picks = jnp.arange(peers * capacity, dtype=jnp.int32)[:, None] == target[None, :]
    outgoing = jnp.dot(
        picks.astype(jnp.bfloat16), hidden, preferred_element_type=jnp.float32
    ).astype(jnp.bfloat16)
    outgoing_slots = jnp.sum(
        jnp.where(picks, (own_slots % resident)[None, :].astype(jnp.float32) + 1.0, 0.0), axis=1
    ) - 1.0

    def swap(value):
        return lax.all_to_all(
            value.reshape((peers, capacity) + value.shape[1:]), "dp", 0, 0, tiled=True
        ).reshape((peers * capacity,) + value.shape[1:])

    rows = swap(outgoing)
    slots = swap(outgoing_slots).astype(jnp.int32)
    ranks = lax.dot_general(rows, down, LAST, preferred_element_type=jnp.float32)
    selector = slots[:, None] == jnp.arange(resident, dtype=jnp.int32)[None, :]
    low = jnp.sum(
        jnp.where(selector[:, :, None], ranks.reshape(-1, resident, rank), 0.0), axis=1
    )
    low = (low + lax.ppermute(low, "tensor", [(0, 1), (1, 0)])).astype(jnp.bfloat16)
    spread = jnp.where(selector[:, :, None], low[:, None, :], jnp.zeros((), jnp.bfloat16))
    update = jnp.dot(
        spread.reshape(-1, resident * rank), up, preferred_element_type=jnp.float32
    ).astype(jnp.bfloat16)
    return swap(update)[target].astype(jnp.float32)


def on_device(
    normed_hidden_states,
    value_base_matrix,
    down_factor_slots,
    up_factor_slots,
    row_adapter_index,
    adapter_slot_table,
):
    resident, rank, width = down_factor_slots.shape
    partial_sum = jnp.dot(
        normed_hidden_states, value_base_matrix, preferred_element_type=jnp.float32
    )
    base_sum = lax.psum_scatter(partial_sum, "tensor", scatter_dimension=1, tiled=True)
    relay = line_relay if lax.axis_size("dp") == 8 else all_to_all_relay
    adapter_update = relay(
        normed_hidden_states,
        down_factor_slots.reshape(resident * rank, width),
        up_factor_slots.reshape(resident * rank, -1),
        row_adapter_index,
        adapter_slot_table,
        rank,
    )
    return (base_sum + adapter_update).astype(jnp.bfloat16)


def solution(mesh):
    placed = (
        P(("groups", "dp"), "tensor"),
        P("tensor", None),
        P(("groups", "dp"), None, "tensor"),
        P(("groups", "dp"), None, "tensor"),
        P(("groups", "dp")),
        P("groups"),
    )
    return jax.shard_map(
        on_device,
        mesh=mesh,
        in_specs=placed,
        out_specs=P(("groups", "dp"), "tensor"),
        check_vma=False,
    )
```

```python
import functools

import jax
import jax.numpy as jnp
from jax import lax
from jax.experimental import pallas as pl
from jax.experimental.pallas import tpu as pltpu
from jax.sharding import PartitionSpec as P

SLOTS_A_STEP = 8
VMEM_BYTES = 20 * 1024 * 1024
LAST = (((1,), (1,)), ((), ()))
FIRST = (((0,), (0,)), ((), ()))


def ranks_kernel(layout, rank, held_ref, *refs):
    pieces = refs[: len(layout)]
    slot_ref, factors_ref, out_ref, rows_ref = refs[len(layout) :]
    step = pl.program_id(0)
    slots = factors_ref.shape[0] // rank

    @pl.when(step == 0)
    def _():
        out_ref[...] = jnp.zeros_like(out_ref)

    @pl.when((held_ref[0] != 0) & (step == 0))
    def _():
        for (row, column), piece in zip(layout, pieces):
            height, width = piece.shape
            rows_ref[row : row + height, column : column + width] = piece[...]

    @pl.when(held_ref[0] != 0)
    def _():
        products = lax.dot_general(
            factors_ref[...], rows_ref[...], LAST, preferred_element_type=jnp.float32
        )
        slot_of_row = slot_ref[...]
        kept = out_ref[...]
        for slot in range(slots):
            kept = jnp.where(
                slot_of_row == step * slots + slot, products[slot * rank : (slot + 1) * rank], kept
            )
        out_ref[...] = kept


def picked_ranks(pieces, slots, factors, rank, column_block=0, held=True):
    total_rows = slots.shape[0]
    width = max(column + piece.shape[1] for _, column, piece in pieces)
    height = SLOTS_A_STEP * rank
    whole = lambda step, held: (0, 0)
    grid_spec = pltpu.PrefetchScalarGridSpec(
        num_scalar_prefetch=1,
        grid=(factors.shape[0] // height,),
        in_specs=[pl.BlockSpec(piece.shape, whole) for _, _, piece in pieces]
        + [
            pl.BlockSpec((1, total_rows), whole),
            pl.BlockSpec((height, width), lambda step, held: (step * held[0], column_block)),
        ],
        out_specs=pl.BlockSpec((rank, total_rows), whole),
        scratch_shapes=[pltpu.VMEM((total_rows, width), jnp.bfloat16)],
    )
    return pl.pallas_call(
        functools.partial(ranks_kernel, [(row, column) for row, column, _ in pieces], rank),
        grid_spec=grid_spec,
        out_shape=jax.ShapeDtypeStruct((rank, total_rows), jnp.float32),
        compiler_params=pltpu.CompilerParams(vmem_limit_bytes=VMEM_BYTES),
        cost_estimate=pl.CostEstimate(flops=0, bytes_accessed=0, transcendentals=0),
    )(
        jnp.asarray(held, jnp.int32)[None],
        *[piece for _, _, piece in pieces],
        slots[None, :],
        factors,
    )


def updates_kernel(own_ref, peer_ref, slot_ref, factors_ref, out_ref):
    rank = own_ref.shape[0]
    low = (own_ref[...] + peer_ref[...]).astype(jnp.bfloat16).astype(jnp.float32)
    slot_of_row = slot_ref[...]
    spread = jnp.concatenate(
        [
            jnp.where(slot_of_row == slot, low, 0.0).astype(jnp.bfloat16)
            for slot in range(factors_ref.shape[0] // rank)
        ],
        axis=0,
    )
    out_ref[...] = lax.dot_general(
        spread, factors_ref[...], FIRST, preferred_element_type=jnp.float32
    ).astype(out_ref.dtype)


def other_core(value):
    return lax.ppermute(value, "tensor", [(0, 1), (1, 0)])


def row_updates(partial_low, slots, factors):
    other = other_core(partial_low)
    rows, columns = slots.shape[0], factors.shape[1]
    return pl.pallas_call(
        updates_kernel,
        out_shape=jax.ShapeDtypeStruct((rows, columns), jnp.bfloat16),
        in_specs=[pl.BlockSpec(memory_space=pltpu.VMEM)] * 4,
        out_specs=pl.BlockSpec(memory_space=pltpu.VMEM),
        compiler_params=pltpu.CompilerParams(vmem_limit_bytes=VMEM_BYTES),
        cost_estimate=pl.CostEstimate(flops=0, bytes_accessed=0, transcendentals=0),
    )(partial_low, other, slots[None, :], factors)


def looked_up(ids, table):
    hits = ids[..., None] == jnp.arange(table.shape[0], dtype=jnp.int32)
    return jnp.sum(jnp.where(hits, table, 0), axis=-1)


def after(value, *others):
    return lax.optimization_barrier((value, *others))[0]


def line_relay(hidden, base_of, down, up, own_ids, table, rank):
    row_count, width = hidden.shape
    resident = down.shape[0] // rank
    capacity = 4 * row_count // lax.axis_size("dp")
    half = width // 2
    me = lax.axis_index("dp")
    devices = range(8)

    def exchange(value, flip):
        return lax.ppermute(value, "dp", [(i, i ^ flip) for i in devices])

    def middle(value):
        return lax.ppermute(value, "dp", [(i, i ^ 6) for i in devices if i // 2 in (1, 2)])

    def outward(value, flip=0):
        return lax.ppermute(value, "dp", [(i, i ^ 2 ^ flip) for i in devices if i // 2 in (1, 2)])

    one, mid = exchange(hidden, 2), middle(hidden)

    place = {}

    def route(slots, pairs):
        rows = jnp.stack([slots[source] // resident for source, _ in pairs])
        hit = rows == jnp.stack([me ^ owner for _, owner in pairs])[:, None]
        places = jnp.where(hit, jnp.cumsum(hit.astype(jnp.int32), axis=1) - 1, -1)
        place.update({pair: places[n] for n, pair in enumerate(pairs)})

    order = jnp.arange(capacity, dtype=jnp.int32)[:, None]

    def one_hot(place):
        return (order == place[None, :]).astype(jnp.bfloat16)

    def compact(place, piece):
        return jnp.dot(one_hot(place), piece, preferred_element_type=jnp.float32).astype(
            jnp.bfloat16
        )

    def middle_across(value):
        return lax.ppermute(value, "dp", [(i, i ^ 1) for i in devices if i // 2 in (1, 2)])

    def split_rows(source, rows, *earlier, move=lambda value: exchange(value, 1)):
        pair = compact(after(place[source, 1], *earlier), rows)
        mine = compact(after(place[source, 0], pair), rows)
        return [(0, 0, mine), (capacity, 0, move(pair))]

    own_slots = looked_up(own_ids, table)[None, :]
    route(own_slots, [(0, owner) for owner in devices])
    rows_0 = split_rows(0, hidden)
    ids = jnp.broadcast_to(after(own_ids, rows_0[0][2]), (8, 1, row_count))
    ids = lax.all_to_all(ids, "dp", 0, 0, tiled=True)

    edge = (me // 2 == 0) | (me // 2 == 3)
    two_edge, two_middle = outward(mid), middle(one)

    own_slots = other_core(after(own_slots, one, mid, rows_0[1][2]))
    ids = after(ids, own_slots).reshape(2, 2, 2, row_count)
    for axis, bit in enumerate((4, 2, 1)):
        ids = jnp.where(me & bit != 0, jnp.flip(ids, axis), ids)
    slots = looked_up(ids.reshape(8, row_count), table)
    slots = jnp.concatenate([own_slots, slots[1:]])
    route(
        slots,
        [(1, 0), (2, 0), (2, 1), (3, 0), (4, 0), (4, 1), (4, 2), (4, 3), (5, 0), (6, 0), (6, 1), (7, 0)],
    )
    local = slots % resident

    def compact_slots(source):
        return jnp.concatenate(
            [
                jnp.sum(jnp.where(order == place[f, 0][None, :], local[f][None, :] + 1, 0), axis=1) - 1
                for f in (source, source ^ 1)
            ]
        )

    rows_1 = split_rows(2, one)
    slots_0, slots_1, slots_2, slots_3 = (compact_slots(source) for source in (0, 2, 4, 6))
    rows_mid = split_rows(6, mid, rows_1[0][2], move=middle_across)
    base = base_of(rows_mid[0][2])
    low_0 = picked_ranks(rows_0, after(slots_0, rows_mid[0][2]), down, rank)
    update_0 = row_updates(low_0, slots_0, up)
    back = {0: update_0[:capacity], 1: exchange(update_0[capacity:], 1)}
    low_1 = picked_ranks(rows_1, after(slots_1, low_0), down, rank)

    straight = compact(after(place[4, 2], low_1), two_middle)
    two = jnp.where(edge, two_edge, two_middle)
    pair = compact(after(place[4, 1], straight), two)
    update_1 = row_updates(after(low_1, pair), slots_1, up)
    across = compact(after(place[4, 3], update_1), two_middle)
    mine = compact(after(place[4, 0], across), two)
    rows_2 = [(0, 0, mine), (capacity, 0, exchange(pair, 1))]
    rows_3 = [(0, 0, outward(straight)), (capacity, 0, outward(across, 1))]

    low_2 = picked_ranks(rows_2, after(slots_2, mine), down, rank)
    update_2 = row_updates(low_2, slots_2, up)
    early = after(update_1, update_2)
    back[2], back[3] = exchange(early[:capacity], 2), exchange(early[capacity:], 3)
    back[4], back[5] = exchange(update_2[:capacity], 4), exchange(update_2[capacity:], 5)

    low_mid = picked_ranks(rows_mid, after(slots_3, update_2), down, rank, 0, ~edge)
    low_3 = picked_ranks(rows_3, after(slots_3, low_mid), down, rank, 0, edge)
    low_3 = after(low_mid + low_3, back[2], back[3], back[4], back[5])
    update_3 = row_updates(low_3, slots_3, up)
    back[6], back[7] = exchange(update_3[:capacity], 6), exchange(update_3[capacity:], 7)

    def spread_back(owners, *others):
        return lax.dot_general(
            jnp.concatenate([one_hot(place[0, owner]) for owner in owners]),
            jnp.concatenate([after(back[owner], *others) for owner in owners]),
            FIRST,
            preferred_element_type=jnp.float32,
        )

    return base + (spread_back(range(6), update_3) + spread_back((6, 7)))


def all_to_all_relay(hidden, base_of, down, up, own_ids, table, rank):
    row_count = hidden.shape[0]
    peers = lax.axis_size("dp")
    resident = down.shape[0] // rank
    capacity = 4 * row_count // peers
    own_slots = looked_up(own_ids, table)
    hits = (own_slots // resident)[:, None] == jnp.arange(peers, dtype=jnp.int32)[None, :]
    place = jnp.sum(jnp.cumsum(hits.astype(jnp.int32), axis=0) * hits, axis=1) - 1
    target = (own_slots // resident) * capacity + place
    picks = jnp.arange(peers * capacity, dtype=jnp.int32)[:, None] == target[None, :]
    outgoing = jnp.dot(
        picks.astype(jnp.bfloat16), hidden, preferred_element_type=jnp.float32
    ).astype(jnp.bfloat16)
    outgoing_slots = jnp.sum(
        jnp.where(picks, (own_slots % resident)[None, :].astype(jnp.float32) + 1.0, 0.0), axis=1
    ) - 1.0

    def swap(value):
        return lax.all_to_all(
            value.reshape((peers, capacity) + value.shape[1:]), "dp", 0, 0, tiled=True
        ).reshape((peers * capacity,) + value.shape[1:])

    rows = swap(outgoing)
    slots = swap(outgoing_slots).astype(jnp.int32)
    ranks = lax.dot_general(rows, down, LAST, preferred_element_type=jnp.float32)
    selector = slots[:, None] == jnp.arange(resident, dtype=jnp.int32)[None, :]
    low = jnp.sum(
        jnp.where(selector[:, :, None], ranks.reshape(-1, resident, rank), 0.0), axis=1
    )
    low = (low + lax.ppermute(low, "tensor", [(0, 1), (1, 0)])).astype(jnp.bfloat16)
    spread = jnp.where(selector[:, :, None], low[:, None, :], jnp.zeros((), jnp.bfloat16))
    update = jnp.dot(
        spread.reshape(-1, resident * rank), up, preferred_element_type=jnp.float32
    ).astype(jnp.bfloat16)
    return base_of(rows) + swap(update)[target].astype(jnp.float32)


def on_device(
    normed_hidden_states,
    value_base_matrix,
    down_factor_slots,
    up_factor_slots,
    row_adapter_index,
    adapter_slot_table,
):
    resident, rank, width = down_factor_slots.shape

    def base_of(*earlier):
        matrix = after(value_base_matrix, *earlier)
        partial_sum = jnp.dot(normed_hidden_states, matrix, preferred_element_type=jnp.float32)
        return lax.psum_scatter(partial_sum, "tensor", scatter_dimension=1, tiled=True)

    relay = line_relay if lax.axis_size("dp") == 8 else all_to_all_relay
    return relay(
        normed_hidden_states,
        base_of,
        down_factor_slots.reshape(resident * rank, width),
        up_factor_slots.reshape(resident * rank, -1),
        row_adapter_index,
        adapter_slot_table,
        rank,
    ).astype(jnp.bfloat16)


def solution(mesh):
    placed = (
        P(("groups", "dp"), "tensor"),
        P("tensor", None),
        P(("groups", "dp"), None, "tensor"),
        P(("groups", "dp"), None, "tensor"),
        P(("groups", "dp")),
        P("groups"),
    )
    return jax.shard_map(
        on_device,
        mesh=mesh,
        in_specs=placed,
        out_specs=P(("groups", "dp"), "tensor"),
        check_vma=False,
    )
```

```python
import functools

import jax
import jax.numpy as jnp
from jax import lax
from jax.experimental import pallas as pl
from jax.experimental.pallas import tpu as pltpu
from jax.sharding import PartitionSpec as P

SLOTS_A_STEP = 8
VMEM_BYTES = 20 * 1024 * 1024
LAST = (((1,), (1,)), ((), ()))
FIRST = (((0,), (0,)), ((), ()))


def ranks_kernel(layout, rank, held_ref, *refs):
    pieces = refs[: len(layout)]
    slot_ref, factors_ref, out_ref, rows_ref = refs[len(layout) :]
    step = pl.program_id(0)
    slots = factors_ref.shape[0] // rank

    @pl.when(step == 0)
    def _():
        out_ref[...] = jnp.zeros_like(out_ref)

    @pl.when((held_ref[0] != 0) & (step == 0))
    def _():
        for (row, column), piece in zip(layout, pieces):
            height, width = piece.shape
            rows_ref[row : row + height, column : column + width] = piece[...]

    @pl.when(held_ref[0] != 0)
    def _():
        products = lax.dot_general(
            factors_ref[...], rows_ref[...], LAST, preferred_element_type=jnp.float32
        )
        slot_of_row = slot_ref[...]
        kept = out_ref[...]
        for slot in range(slots):
            kept = jnp.where(
                slot_of_row == step * slots + slot, products[slot * rank : (slot + 1) * rank], kept
            )
        out_ref[...] = kept


def picked_ranks(pieces, slots, factors, rank, column_block=0, held=True):
    total_rows = slots.shape[0]
    width = max(column + piece.shape[1] for _, column, piece in pieces)
    height = SLOTS_A_STEP * rank
    whole = lambda step, held: (0, 0)
    grid_spec = pltpu.PrefetchScalarGridSpec(
        num_scalar_prefetch=1,
        grid=(factors.shape[0] // height,),
        in_specs=[pl.BlockSpec(piece.shape, whole) for _, _, piece in pieces]
        + [
            pl.BlockSpec((1, total_rows), whole),
            pl.BlockSpec((height, width), lambda step, held: (step * held[0], column_block)),
        ],
        out_specs=pl.BlockSpec((rank, total_rows), whole),
        scratch_shapes=[pltpu.VMEM((total_rows, width), jnp.bfloat16)],
    )
    return pl.pallas_call(
        functools.partial(ranks_kernel, [(row, column) for row, column, _ in pieces], rank),
        grid_spec=grid_spec,
        out_shape=jax.ShapeDtypeStruct((rank, total_rows), jnp.float32),
        compiler_params=pltpu.CompilerParams(vmem_limit_bytes=VMEM_BYTES),
        cost_estimate=pl.CostEstimate(flops=0, bytes_accessed=0, transcendentals=0),
    )(
        jnp.asarray(held, jnp.int32)[None],
        *[piece for _, _, piece in pieces],
        slots[None, :],
        factors,
    )


def updates_kernel(own_ref, peer_ref, slot_ref, factors_ref, out_ref):
    rank = own_ref.shape[0]
    low = (own_ref[...] + peer_ref[...]).astype(jnp.bfloat16).astype(jnp.float32)
    slot_of_row = slot_ref[...]
    spread = jnp.concatenate(
        [
            jnp.where(slot_of_row == slot, low, 0.0).astype(jnp.bfloat16)
            for slot in range(factors_ref.shape[0] // rank)
        ],
        axis=0,
    )
    out_ref[...] = lax.dot_general(
        spread, factors_ref[...], FIRST, preferred_element_type=jnp.float32
    ).astype(out_ref.dtype)


def other_core(value):
    return lax.ppermute(value, "tensor", [(0, 1), (1, 0)])


def row_updates(partial_low, slots, factors):
    other = other_core(partial_low)
    rows, columns = slots.shape[0], factors.shape[1]
    return pl.pallas_call(
        updates_kernel,
        out_shape=jax.ShapeDtypeStruct((rows, columns), jnp.bfloat16),
        in_specs=[pl.BlockSpec(memory_space=pltpu.VMEM)] * 4,
        out_specs=pl.BlockSpec(memory_space=pltpu.VMEM),
        compiler_params=pltpu.CompilerParams(vmem_limit_bytes=VMEM_BYTES),
        cost_estimate=pl.CostEstimate(flops=0, bytes_accessed=0, transcendentals=0),
    )(partial_low, other, slots[None, :], factors)


def base_kernel(rows_ref, matrix_ref, out_ref):
    out_ref[...] = jnp.dot(rows_ref[...], matrix_ref[...], preferred_element_type=jnp.float32)


def base_product(rows, matrix):
    block = matrix.shape[1] // 4
    return pl.pallas_call(
        base_kernel,
        grid=(4,),
        out_shape=jax.ShapeDtypeStruct((rows.shape[0], matrix.shape[1]), jnp.float32),
        in_specs=[
            pl.BlockSpec(rows.shape, lambda step: (0, 0)),
            pl.BlockSpec((matrix.shape[0], block), lambda step: (0, step)),
        ],
        out_specs=pl.BlockSpec((rows.shape[0], block), lambda step: (0, step)),
        compiler_params=pltpu.CompilerParams(vmem_limit_bytes=VMEM_BYTES),
        cost_estimate=pl.CostEstimate(flops=0, bytes_accessed=0, transcendentals=0),
    )(rows, matrix)


def looked_up(ids, table):
    hits = ids[..., None] == jnp.arange(table.shape[0], dtype=jnp.int32)
    return jnp.sum(jnp.where(hits, table, 0), axis=-1)


def after(value, *others):
    return lax.optimization_barrier((value, *others))[0]


def line_relay(hidden, matrix, down, up, own_ids, table, rank):
    row_count, width = hidden.shape
    resident = down.shape[0] // rank
    capacity = 4 * row_count // lax.axis_size("dp")
    half = width // 2
    me = lax.axis_index("dp")
    devices = range(8)

    def exchange(value, flip):
        return lax.ppermute(value, "dp", [(i, i ^ flip) for i in devices])

    def middle(value):
        return lax.ppermute(value, "dp", [(i, i ^ 6) for i in devices if i // 2 in (1, 2)])

    def outward(value, flip=0):
        return lax.ppermute(value, "dp", [(i, i ^ 2 ^ flip) for i in devices if i // 2 in (1, 2)])

    one, mid = exchange(hidden, 2), middle(hidden)

    place = {}

    def route(slots, pairs):
        rows = jnp.stack([slots[source] // resident for source, _ in pairs])
        hit = rows == jnp.stack([me ^ owner for _, owner in pairs])[:, None]
        places = jnp.where(hit, jnp.cumsum(hit.astype(jnp.int32), axis=1) - 1, -1)
        place.update({pair: places[n] for n, pair in enumerate(pairs)})

    order = jnp.arange(capacity, dtype=jnp.int32)[:, None]

    def one_hot(place):
        return (order == place[None, :]).astype(jnp.bfloat16)

    def compact(place, piece):
        return jnp.dot(one_hot(place), piece, preferred_element_type=jnp.float32).astype(
            jnp.bfloat16
        )

    def middle_across(value):
        return lax.ppermute(value, "dp", [(i, i ^ 1) for i in devices if i // 2 in (1, 2)])

    def split_rows(source, rows, *earlier, move=lambda value: exchange(value, 1)):
        pair = compact(after(place[source, 1], *earlier), rows)
        mine = compact(after(place[source, 0], pair), rows)
        return [(0, 0, mine), (capacity, 0, move(pair))]

    own_slots = looked_up(own_ids, table)[None, :]
    route(own_slots, [(0, owner) for owner in devices])
    rows_0 = split_rows(0, hidden)
    ids = jnp.broadcast_to(after(own_ids, rows_0[0][2]), (8, 1, row_count))
    ids = lax.all_to_all(ids, "dp", 0, 0, tiled=True)

    partial_base = base_product(hidden, after(matrix, rows_0[0][2]))
    base = lax.psum_scatter(partial_base, "tensor", scatter_dimension=1, tiled=True)

    edge = (me // 2 == 0) | (me // 2 == 3)
    two_edge, two_middle = outward(mid), middle(one)

    own_slots = other_core(after(own_slots, one, mid, rows_0[1][2], partial_base))
    ids = after(ids, own_slots).reshape(2, 2, 2, row_count)
    for axis, bit in enumerate((4, 2, 1)):
        ids = jnp.where(me & bit != 0, jnp.flip(ids, axis), ids)
    slots = looked_up(ids.reshape(8, row_count), table)
    slots = jnp.concatenate([own_slots, slots[1:]])
    route(
        slots,
        [(1, 0), (2, 0), (2, 1), (3, 0), (4, 0), (4, 1), (4, 2), (4, 3), (5, 0), (6, 0), (6, 1), (7, 0)],
    )
    local = slots % resident

    def compact_slots(source):
        return jnp.concatenate(
            [
                jnp.sum(jnp.where(order == place[f, 0][None, :], local[f][None, :] + 1, 0), axis=1) - 1
                for f in (source, source ^ 1)
            ]
        )

    rows_1 = split_rows(2, one)
    slots_0, slots_1, slots_2, slots_3 = (compact_slots(source) for source in (0, 2, 4, 6))
    rows_mid = split_rows(6, mid, rows_1[0][2], move=middle_across)
    low_0 = picked_ranks(rows_0, after(slots_0, rows_mid[0][2]), down, rank)
    update_0 = row_updates(low_0, slots_0, up)
    back = {0: update_0[:capacity]}
    low_1 = picked_ranks(rows_1, after(slots_1, low_0), down, rank)

    straight = compact(after(place[4, 2], low_1), two_middle)
    two = jnp.where(edge, two_edge, two_middle)
    pair = compact(after(place[4, 1], straight), two)
    update_1 = row_updates(after(low_1, pair), slots_1, up)
    across = compact(after(place[4, 3], update_1), two_middle)
    mine = compact(after(place[4, 0], across), two)
    rows_2 = [(0, 0, mine), (capacity, 0, exchange(pair, 1))]
    rows_3 = [(0, 0, outward(straight)), (capacity, 0, outward(across, 1))]

    low_2 = picked_ranks(rows_2, after(slots_2, mine), down, rank)
    update_2 = row_updates(low_2, slots_2, up)
    back[1] = exchange(after(update_0, update_2)[capacity:], 1)
    early = after(update_1, update_2)
    back[2], back[3] = exchange(early[:capacity], 2), exchange(early[capacity:], 3)
    back[4], back[5] = exchange(update_2[:capacity], 4), exchange(update_2[capacity:], 5)

    low_mid = picked_ranks(rows_mid, after(slots_3, update_2), down, rank, 0, ~edge)
    low_3 = picked_ranks(rows_3, after(slots_3, low_mid), down, rank, 0, edge)
    low_3 = after(low_mid + low_3, back[1], back[2], back[3], back[4], back[5])
    update_3 = row_updates(low_3, slots_3, up)
    back[6], back[7] = exchange(update_3[:capacity], 6), exchange(update_3[capacity:], 7)

    def spread_back(owners, *others):
        return lax.dot_general(
            jnp.concatenate([one_hot(place[0, owner]) for owner in owners]),
            jnp.concatenate([after(back[owner], *others) for owner in owners]),
            FIRST,
            preferred_element_type=jnp.float32,
        )

    return base + (spread_back(range(6), update_3) + spread_back((6, 7)))


def all_to_all_relay(hidden, matrix, down, up, own_ids, table, rank):
    row_count = hidden.shape[0]
    peers = lax.axis_size("dp")
    resident = down.shape[0] // rank
    capacity = 4 * row_count // peers
    own_slots = looked_up(own_ids, table)
    hits = (own_slots // resident)[:, None] == jnp.arange(peers, dtype=jnp.int32)[None, :]
    place = jnp.sum(jnp.cumsum(hits.astype(jnp.int32), axis=0) * hits, axis=1) - 1
    target = (own_slots // resident) * capacity + place
    picks = jnp.arange(peers * capacity, dtype=jnp.int32)[:, None] == target[None, :]
    outgoing = jnp.dot(
        picks.astype(jnp.bfloat16), hidden, preferred_element_type=jnp.float32
    ).astype(jnp.bfloat16)
    outgoing_slots = jnp.sum(
        jnp.where(picks, (own_slots % resident)[None, :].astype(jnp.float32) + 1.0, 0.0), axis=1
    ) - 1.0

    def swap(value):
        return lax.all_to_all(
            value.reshape((peers, capacity) + value.shape[1:]), "dp", 0, 0, tiled=True
        ).reshape((peers * capacity,) + value.shape[1:])

    rows = swap(outgoing)
    slots = swap(outgoing_slots).astype(jnp.int32)
    ranks = lax.dot_general(rows, down, LAST, preferred_element_type=jnp.float32)
    selector = slots[:, None] == jnp.arange(resident, dtype=jnp.int32)[None, :]
    low = jnp.sum(
        jnp.where(selector[:, :, None], ranks.reshape(-1, resident, rank), 0.0), axis=1
    )
    low = (low + lax.ppermute(low, "tensor", [(0, 1), (1, 0)])).astype(jnp.bfloat16)
    spread = jnp.where(selector[:, :, None], low[:, None, :], jnp.zeros((), jnp.bfloat16))
    update = jnp.dot(
        spread.reshape(-1, resident * rank), up, preferred_element_type=jnp.float32
    ).astype(jnp.bfloat16)
    base = jnp.dot(hidden, matrix, preferred_element_type=jnp.float32)
    base = lax.psum_scatter(base, "tensor", scatter_dimension=1, tiled=True)
    return base + swap(update)[target].astype(jnp.float32)


def on_device(
    normed_hidden_states,
    value_base_matrix,
    down_factor_slots,
    up_factor_slots,
    row_adapter_index,
    adapter_slot_table,
):
    resident, rank, width = down_factor_slots.shape

    relay = line_relay if lax.axis_size("dp") == 8 else all_to_all_relay
    return relay(
        normed_hidden_states,
        value_base_matrix,
        down_factor_slots.reshape(resident * rank, width),
        up_factor_slots.reshape(resident * rank, -1),
        row_adapter_index,
        adapter_slot_table,
        rank,
    ).astype(jnp.bfloat16)


def solution(mesh):
    placed = (
        P(("groups", "dp"), "tensor"),
        P("tensor", None),
        P(("groups", "dp"), None, "tensor"),
        P(("groups", "dp"), None, "tensor"),
        P(("groups", "dp")),
        P("groups"),
    )
    return jax.shard_map(
        on_device,
        mesh=mesh,
        in_specs=placed,
        out_specs=P(("groups", "dp"), "tensor"),
        check_vma=False,
    )
```

```python
import functools

import jax
import jax.numpy as jnp
from jax import lax
from jax.experimental import pallas as pl
from jax.experimental.pallas import tpu as pltpu
from jax.sharding import PartitionSpec as P

SLOTS_A_STEP = 8
VMEM_BYTES = 20 * 1024 * 1024
LAST = (((1,), (1,)), ((), ()))
FIRST = (((0,), (0,)), ((), ()))


def ranks_kernel(layout, rank, held_ref, *refs):
    pieces = refs[: len(layout)]
    slot_ref, factors_ref, out_ref, rows_ref = refs[len(layout) :]
    step = pl.program_id(0)
    slots = factors_ref.shape[0] // rank

    @pl.when(step == 0)
    def _():
        out_ref[...] = jnp.zeros_like(out_ref)

    @pl.when((held_ref[0] != 0) & (step == 0))
    def _():
        for (row, column), piece in zip(layout, pieces):
            height, width = piece.shape
            rows_ref[row : row + height, column : column + width] = piece[...]

    @pl.when(held_ref[0] != 0)
    def _():
        products = lax.dot_general(
            factors_ref[...], rows_ref[...], LAST, preferred_element_type=jnp.float32
        )
        slot_of_row = slot_ref[...]
        kept = out_ref[...]
        for slot in range(slots):
            kept = jnp.where(
                slot_of_row == step * slots + slot, products[slot * rank : (slot + 1) * rank], kept
            )
        out_ref[...] = kept


def picked_ranks(pieces, slots, factors, rank, column_block=0, held=True):
    total_rows = slots.shape[0]
    width = max(column + piece.shape[1] for _, column, piece in pieces)
    height = SLOTS_A_STEP * rank
    whole = lambda step, held: (0, 0)
    grid_spec = pltpu.PrefetchScalarGridSpec(
        num_scalar_prefetch=1,
        grid=(factors.shape[0] // height,),
        in_specs=[pl.BlockSpec(piece.shape, whole) for _, _, piece in pieces]
        + [
            pl.BlockSpec((1, total_rows), whole),
            pl.BlockSpec((height, width), lambda step, held: (step * held[0], column_block)),
        ],
        out_specs=pl.BlockSpec((rank, total_rows), whole),
        scratch_shapes=[pltpu.VMEM((total_rows, width), jnp.bfloat16)],
    )
    return pl.pallas_call(
        functools.partial(ranks_kernel, [(row, column) for row, column, _ in pieces], rank),
        grid_spec=grid_spec,
        out_shape=jax.ShapeDtypeStruct((rank, total_rows), jnp.float32),
        compiler_params=pltpu.CompilerParams(vmem_limit_bytes=VMEM_BYTES),
        cost_estimate=pl.CostEstimate(flops=0, bytes_accessed=0, transcendentals=0),
    )(
        jnp.asarray(held, jnp.int32)[None],
        *[piece for _, _, piece in pieces],
        slots[None, :],
        factors,
    )


def updates_kernel(own_ref, peer_ref, slot_ref, factors_ref, out_ref):
    rank = own_ref.shape[0]
    low = (own_ref[...] + peer_ref[...]).astype(jnp.bfloat16).astype(jnp.float32)
    slot_of_row = slot_ref[...]
    spread = jnp.concatenate(
        [
            jnp.where(slot_of_row == slot, low, 0.0).astype(jnp.bfloat16)
            for slot in range(factors_ref.shape[0] // rank)
        ],
        axis=0,
    )
    out_ref[...] = lax.dot_general(
        spread, factors_ref[...], FIRST, preferred_element_type=jnp.float32
    ).astype(out_ref.dtype)


def other_core(value):
    return lax.ppermute(value, "tensor", [(0, 1), (1, 0)])


def row_updates(partial_low, slots, factors):
    other = other_core(partial_low)
    rows, columns = slots.shape[0], factors.shape[1]
    return pl.pallas_call(
        updates_kernel,
        out_shape=jax.ShapeDtypeStruct((rows, columns), jnp.bfloat16),
        in_specs=[pl.BlockSpec(memory_space=pltpu.VMEM)] * 4,
        out_specs=pl.BlockSpec(memory_space=pltpu.VMEM),
        compiler_params=pltpu.CompilerParams(vmem_limit_bytes=VMEM_BYTES),
        cost_estimate=pl.CostEstimate(flops=0, bytes_accessed=0, transcendentals=0),
    )(partial_low, other, slots[None, :], factors)


def base_kernel(rows_ref, matrix_ref, out_ref):
    out_ref[...] = jnp.dot(rows_ref[...], matrix_ref[...], preferred_element_type=jnp.float32)


def base_product(rows, matrix):
    block = matrix.shape[1] // 4
    return pl.pallas_call(
        base_kernel,
        grid=(4,),
        out_shape=jax.ShapeDtypeStruct((rows.shape[0], matrix.shape[1]), jnp.float32),
        in_specs=[
            pl.BlockSpec(rows.shape, lambda step: (0, 0)),
            pl.BlockSpec((matrix.shape[0], block), lambda step: (0, step)),
        ],
        out_specs=pl.BlockSpec((rows.shape[0], block), lambda step: (0, step)),
        compiler_params=pltpu.CompilerParams(vmem_limit_bytes=VMEM_BYTES),
        cost_estimate=pl.CostEstimate(flops=0, bytes_accessed=0, transcendentals=0),
    )(rows, matrix)


def looked_up(ids, table):
    hits = ids[..., None] == jnp.arange(table.shape[0], dtype=jnp.int32)
    return jnp.sum(jnp.where(hits, table, 0), axis=-1)


def after(value, *others):
    return lax.optimization_barrier((value, *others))[0]


def line_relay(hidden, matrix, down, up, own_ids, table, rank):
    row_count, width = hidden.shape
    resident = down.shape[0] // rank
    capacity = 4 * row_count // lax.axis_size("dp")
    half = width // 2
    me = lax.axis_index("dp")
    devices = range(8)

    def exchange(value, flip):
        return lax.ppermute(value, "dp", [(i, i ^ flip) for i in devices])

    def middle(value):
        return lax.ppermute(value, "dp", [(i, i ^ 6) for i in devices if i // 2 in (1, 2)])

    def outward(value, flip=0):
        return lax.ppermute(value, "dp", [(i, i ^ 2 ^ flip) for i in devices if i // 2 in (1, 2)])

    one, mid = exchange(hidden, 2), middle(hidden)

    place = {}

    def route(slots, pairs):
        rows = jnp.stack([slots[source] // resident for source, _ in pairs])
        hit = rows == jnp.stack([me ^ owner for _, owner in pairs])[:, None]
        places = jnp.where(hit, jnp.cumsum(hit.astype(jnp.int32), axis=1) - 1, -1)
        place.update({pair: places[n] for n, pair in enumerate(pairs)})

    order = jnp.arange(capacity, dtype=jnp.int32)[:, None]

    def one_hot(place):
        return (order == place[None, :]).astype(jnp.bfloat16)

    def compact(place, piece):
        return jnp.dot(one_hot(place), piece, preferred_element_type=jnp.float32).astype(
            jnp.bfloat16
        )

    def middle_across(value):
        return lax.ppermute(value, "dp", [(i, i ^ 1) for i in devices if i // 2 in (1, 2)])

    def split_rows(source, rows, *earlier, move=lambda value: exchange(value, 1)):
        pair = compact(after(place[source, 1], *earlier), rows)
        mine = compact(after(place[source, 0], pair), rows)
        return [(0, 0, mine), (capacity, 0, move(pair))]

    own_slots = looked_up(own_ids, table)[None, :]
    route(own_slots, [(0, owner) for owner in devices])
    rows_0 = split_rows(0, hidden)
    ids = jnp.broadcast_to(after(own_ids, rows_0[0][2]), (8, 1, row_count))
    ids = lax.all_to_all(ids, "dp", 0, 0, tiled=True)

    partial_base = base_product(hidden, after(matrix, rows_0[0][2]))
    base = lax.psum_scatter(partial_base, "tensor", scatter_dimension=1, tiled=True)

    edge = (me // 2 == 0) | (me // 2 == 3)
    two_edge, two_middle = outward(mid), middle(one)

    own_slots = other_core(after(own_slots, one, mid, rows_0[1][2], partial_base))
    ids = after(ids, own_slots).reshape(2, 2, 2, row_count)
    for axis, bit in enumerate((4, 2, 1)):
        ids = jnp.where(me & bit != 0, jnp.flip(ids, axis), ids)
    slots = looked_up(ids.reshape(8, row_count), table)
    slots = jnp.concatenate([own_slots, slots[1:]])
    route(
        slots,
        [(1, 0), (2, 0), (2, 1), (3, 0), (4, 0), (4, 1), (4, 2), (4, 3), (5, 0), (6, 0), (6, 1), (7, 0)],
    )
    local = slots % resident

    def compact_slots(source):
        return jnp.concatenate(
            [
                jnp.sum(jnp.where(order == place[f, 0][None, :], local[f][None, :] + 1, 0), axis=1) - 1
                for f in (source, source ^ 1)
            ]
        )

    rows_1 = split_rows(2, one)
    slots_0, slots_1, slots_2, slots_3 = (compact_slots(source) for source in (0, 2, 4, 6))
    rows_mid = split_rows(6, mid, rows_1[0][2], move=middle_across)
    low_0 = picked_ranks(rows_0, after(slots_0, rows_mid[0][2]), down, rank)
    update_0 = row_updates(low_0, slots_0, up)
    back = {0: update_0[:capacity]}
    low_1 = picked_ranks(rows_1, after(slots_1, update_0), down, rank)

    straight = compact(after(place[4, 2], low_1), two_middle)
    two = jnp.where(edge, two_edge, two_middle)
    pair = compact(after(place[4, 1], straight), two)
    update_1 = row_updates(after(low_1, pair), slots_1, up)
    across = compact(after(place[4, 3], update_1), two_middle)
    mine = compact(after(place[4, 0], across), two)
    rows_2 = [(0, 0, mine), (capacity, 0, exchange(pair, 1))]
    rows_3 = [(0, 0, outward(straight)), (capacity, 0, outward(across, 1))]

    low_2 = picked_ranks(rows_2, after(slots_2, mine), down, rank)
    update_2 = row_updates(low_2, slots_2, up)
    back[1] = exchange(after(update_0, update_2)[capacity:], 1)
    early = after(update_1, update_2)
    back[2], back[3] = exchange(early[:capacity], 2), exchange(early[capacity:], 3)
    back[4], back[5] = exchange(update_2[:capacity], 4), exchange(update_2[capacity:], 5)

    low_mid = picked_ranks(rows_mid, after(slots_3, update_2), down, rank, 0, ~edge)
    low_3 = picked_ranks(rows_3, after(slots_3, low_mid), down, rank, 0, edge)
    low_3 = after(low_mid + low_3, back[1], back[2], back[3], back[4], back[5])
    update_3 = row_updates(low_3, slots_3, up)
    back[6], back[7] = exchange(update_3[:capacity], 6), exchange(update_3[capacity:], 7)

    def spread_back(owners, *others):
        return lax.dot_general(
            jnp.concatenate([one_hot(place[0, owner]) for owner in owners]),
            jnp.concatenate([after(back[owner], *others) for owner in owners]),
            FIRST,
            preferred_element_type=jnp.float32,
        )

    early = after(base + spread_back(range(6), update_3), update_3)
    return early + spread_back((6, 7))


def all_to_all_relay(hidden, matrix, down, up, own_ids, table, rank):
    row_count = hidden.shape[0]
    peers = lax.axis_size("dp")
    resident = down.shape[0] // rank
    capacity = 4 * row_count // peers
    own_slots = looked_up(own_ids, table)
    hits = (own_slots // resident)[:, None] == jnp.arange(peers, dtype=jnp.int32)[None, :]
    place = jnp.sum(jnp.cumsum(hits.astype(jnp.int32), axis=0) * hits, axis=1) - 1
    target = (own_slots // resident) * capacity + place
    picks = jnp.arange(peers * capacity, dtype=jnp.int32)[:, None] == target[None, :]
    outgoing = jnp.dot(
        picks.astype(jnp.bfloat16), hidden, preferred_element_type=jnp.float32
    ).astype(jnp.bfloat16)
    outgoing_slots = jnp.sum(
        jnp.where(picks, (own_slots % resident)[None, :].astype(jnp.float32) + 1.0, 0.0), axis=1
    ) - 1.0

    def swap(value):
        return lax.all_to_all(
            value.reshape((peers, capacity) + value.shape[1:]), "dp", 0, 0, tiled=True
        ).reshape((peers * capacity,) + value.shape[1:])

    rows = swap(outgoing)
    slots = swap(outgoing_slots).astype(jnp.int32)
    ranks = lax.dot_general(rows, down, LAST, preferred_element_type=jnp.float32)
    selector = slots[:, None] == jnp.arange(resident, dtype=jnp.int32)[None, :]
    low = jnp.sum(
        jnp.where(selector[:, :, None], ranks.reshape(-1, resident, rank), 0.0), axis=1
    )
    low = (low + lax.ppermute(low, "tensor", [(0, 1), (1, 0)])).astype(jnp.bfloat16)
    spread = jnp.where(selector[:, :, None], low[:, None, :], jnp.zeros((), jnp.bfloat16))
    update = jnp.dot(
        spread.reshape(-1, resident * rank), up, preferred_element_type=jnp.float32
    ).astype(jnp.bfloat16)
    base = jnp.dot(hidden, matrix, preferred_element_type=jnp.float32)
    base = lax.psum_scatter(base, "tensor", scatter_dimension=1, tiled=True)
    return base + swap(update)[target].astype(jnp.float32)


def on_device(
    normed_hidden_states,
    value_base_matrix,
    down_factor_slots,
    up_factor_slots,
    row_adapter_index,
    adapter_slot_table,
):
    resident, rank, width = down_factor_slots.shape

    relay = line_relay if lax.axis_size("dp") == 8 else all_to_all_relay
    return relay(
        normed_hidden_states,
        value_base_matrix,
        down_factor_slots.reshape(resident * rank, width),
        up_factor_slots.reshape(resident * rank, -1),
        row_adapter_index,
        adapter_slot_table,
        rank,
    ).astype(jnp.bfloat16)


def solution(mesh):
    placed = (
        P(("groups", "dp"), "tensor"),
        P("tensor", None),
        P(("groups", "dp"), None, "tensor"),
        P(("groups", "dp"), None, "tensor"),
        P(("groups", "dp")),
        P("groups"),
    )
    return jax.shard_map(
        on_device,
        mesh=mesh,
        in_specs=placed,
        out_specs=P(("groups", "dp"), "tensor"),
        check_vma=False,
    )
```
